32 devices in a mesh: ta: 8 (over z, x), sa: 4 (over y, core).
Axes of the slice: x: 2, y: 2, z: 4, core: 2. Of those that a mesh axis runs over, the one named last changes fastest.
Arguments:
- adjoint_in: float32 [3, 2, 48, 8, 64, 128], P(None, None, None, 'sa', 'ta'), may hold values from -6 to 6
- links_late: float32 [4, 3, 3, 2, 8, 64, 128], P(None, None, None, None, 'sa', 'ta'), may hold values from -2.4 to 2.4
- links_mid: float32 [4, 3, 3, 2, 8, 64, 128], P(None, None, None, None, 'sa', 'ta'), may hold values from -2.4 to 2.4
- src_value: float32 [3, 2, 48, 4096], P(None, None, None, ('ta', 'sa')), may hold values from -6 to 6
- src_coord: int32 [4, 4096], P(None, ('ta', 'sa')), may hold values from 0 to 63, as said below
Outputs:
- section_two: float32 [3, 2, 48, 8, 64, 128], P(None, None, None, 'sa', 'ta')
- section_one: float32 [3, 2, 48, 8, 64, 128], P(None, None, None, 'sa', 'ta')
The draws below stay inside these ranges and needn't reach their ends.
Inputs may be any that keep to these rules, and one draw needn't show every extreme that they name: `src_coord`: the 128 records that lie on the device at position i of ta have time coordinates from i * 8 to (i + 1) * 8 - 1. Among the records of one device at most 64 have x coordinates in the planes of one index of sa (x // 2); for every position of ta, some index of sa receives exactly 64 records from every device at that position. Several records may name the same site.
All inputs are finite; a program needn't handle non-finite values.
Results may differ from the reference program's by a relative error of at most 0.0001.
Values sent between devices are 32-bit elements; how exact they have to be, the bound alone decides.
A program may use at most 128 MiB of HBM per device.

```python
import jax
import jax.numpy as jnp
from jax import lax

SPIN_COLS = 48
PLANES_T = 8
PLANES_X = 2
EXTENT_Y = 16
EXTENT_Z = 8
SOURCES_DEV = 128
GLOBAL_T = 64
GLOBAL_X = 8
FACE = 128
SOURCES = 4096
CAPACITY = 64


def draw_src_coord(key, part):
    slab_count = GLOBAL_T // PLANES_T
    group_count = GLOBAL_X // PLANES_X
    hot_key = jax.random.fold_in(key, 11)
    device_key = jax.random.fold_in(key, 12)
    hottest = jax.random.randint(hot_key, (slab_count,), 0, group_count).astype(jnp.int32)

    def one_device(device):
        local_key = jax.random.fold_in(device_key, device)
        keys = jax.random.split(local_key, 6)
        slab_index = device // group_count
        chosen = hottest[slab_index]
        others = (chosen + 1 + jnp.arange(group_count - 1, dtype=jnp.int32)) % group_count
        spread = jax.random.permutation(keys[0], (group_count - 1) * CAPACITY)[:SOURCES_DEV - CAPACITY]
        owners = jnp.concatenate([jnp.full((CAPACITY,), chosen, jnp.int32), others[spread // CAPACITY].astype(jnp.int32)])
        owners = jax.random.permutation(keys[1], owners)
        t_coord = slab_index * PLANES_T + jax.random.randint(keys[2], (SOURCES_DEV,), 0, PLANES_T)
        x_coord = owners * PLANES_X + jax.random.randint(keys[3], (SOURCES_DEV,), 0, PLANES_X)
        y_coord = jax.random.randint(keys[4], (SOURCES_DEV,), 0, EXTENT_Y)
        z_coord = jax.random.randint(keys[5], (SOURCES_DEV,), 0, EXTENT_Z)
        return jnp.stack([t_coord, x_coord, y_coord, z_coord]).astype(jnp.int32)
    stacked = jax.vmap(one_device)(jnp.arange(slab_count * group_count, dtype=jnp.int32))
    return jnp.transpose(stacked, (1, 0, 2)).reshape(4, SOURCES).astype(jnp.int32)


def levels(key, shape, cuts, least, largest):
    gain = 1.0
    for axis_at, parts in cuts:
        steps = jax.random.uniform(jax.random.fold_in(jax.random.fold_in(key, 6), axis_at), (parts,), jnp.float32, least / len(cuts), largest / len(cuts))
        gain = gain * jnp.repeat(jnp.exp(steps), shape[axis_at] // parts).reshape((-1,) + (1,) * (len(shape) - 1 - axis_at))
    return gain


def centred(stream_key, dims, scale, limit, cuts=(), held_as=jnp.bfloat16):
    level = levels(stream_key, dims, cuts, -0.22, 0.18) if cuts else 1.0
    result = jax.random.normal(stream_key, dims, jnp.float32) * scale * level
    return jnp.minimum(jnp.maximum(result, -limit), limit).astype(held_as)


def setup_inputs(seed: int = 0) -> dict:
    splits = jax.random.split(jax.random.key(seed), 6)
    adjoint_in = centred(splits[0], (3, 2, SPIN_COLS, GLOBAL_X, GLOBAL_T, FACE), 1.0, 6.0, ((3, 4), (4, 8)), jnp.float32)
    links_late = centred(splits[1], (4, 3, 3, 2, GLOBAL_X, GLOBAL_T, FACE), 0.4, 2.4, ((4, 4), (5, 8)), jnp.float32)
    links_mid = centred(splits[2], (4, 3, 3, 2, GLOBAL_X, GLOBAL_T, FACE), 0.4, 2.4, ((4, 4), (5, 8)), jnp.float32)
    src_value = centred(splits[3], (3, 2, SPIN_COLS, SOURCES), 1.0, 6.0, ((3, 32),), jnp.float32)
    src_coord = draw_src_coord(jax.random.fold_in(splits[5], 71), 0)
    return dict(adjoint_in=adjoint_in, links_late=links_late, links_mid=links_mid, src_value=src_value, src_coord=src_coord)


flow_step = 0.0625
coef_late = 0.75 * flow_step
coef_mid = 8.0 / 9.0 * flow_step
column_block = 4


def color_mul(matrix, spinor):
    mat_re = matrix[:, :, 0][:, :, None]
    mat_im = matrix[:, :, 1][:, :, None]
    vec_re = spinor[:, 0][None]
    vec_im = spinor[:, 1][None]
    real_part = jnp.sum(mat_re * vec_re - mat_im * vec_im, axis=1)
    imag_part = jnp.sum(mat_re * vec_im + mat_im * vec_re, axis=1)
    return jnp.stack([real_part, imag_part], axis=1)


def dagger(matrix):
    swapped = jnp.swapaxes(matrix, 0, 1)
    return jnp.stack([swapped[:, :, 0], -swapped[:, :, 1]], axis=2)


def laplacian(spinor, matrices):
    time_len = spinor.shape[4]
    time_pos = jnp.arange(time_len)
    sign_up = jnp.where(time_pos == time_len - 1, -1.0, 1.0).astype(spinor.dtype)[:, None, None]
    sign_down = jnp.where(time_pos == 0, -1.0, 1.0).astype(spinor.dtype)[:, None, None]
    running = jnp.zeros_like(spinor)
    for direction, axis_pos in ((0, 4), (1, 3), (2, 5), (3, 6)):
        matrix = matrices[direction]
        forward = jnp.roll(spinor, -1, axis_pos)
        backward = jnp.roll(color_mul(dagger(matrix), spinor), 1, axis_pos)
        if direction == 0:
            forward = forward * sign_up
            backward = backward * sign_down
        running = running + (color_mul(matrix, forward) + backward)
    return running - 8.0 * spinor


def reference(adjoint_in, links_late, links_mid, src_value, src_coord):
    late_grid = links_late.reshape(4, 3, 3, 2, GLOBAL_X, GLOBAL_T, EXTENT_Y, EXTENT_Z)
    mid_grid = links_mid.reshape(4, 3, 3, 2, GLOBAL_X, GLOBAL_T, EXTENT_Y, EXTENT_Z)
    face_index = (src_coord[2] * EXTENT_Z + src_coord[3]).astype(jnp.int32)
    x_index = src_coord[1].astype(jnp.int32)
    t_index = src_coord[0].astype(jnp.int32)

    def one_block(block_index, carry):
        out_two, out_one = carry
        start = (block_index * column_block).astype(jnp.int32)
        adjoint = lax.dynamic_slice_in_dim(adjoint_in, start, column_block, 2)
        sources = lax.dynamic_slice_in_dim(src_value, start, column_block, 2)
        adjoint_top = adjoint.at[:, :, :, x_index, t_index, face_index].add(sources)
        grid_top = adjoint_top.reshape(3, 2, column_block, GLOBAL_X, GLOBAL_T, EXTENT_Y, EXTENT_Z)
        second = coef_late * laplacian(grid_top, late_grid)
        first = grid_top + coef_mid * laplacian(second, mid_grid)
        out_two = lax.dynamic_update_slice_in_dim(out_two, second.reshape(adjoint.shape), start, 2)
        out_one = lax.dynamic_update_slice_in_dim(out_one, first.reshape(adjoint.shape), start, 2)
        return out_two, out_one

    initial = (jnp.zeros_like(adjoint_in), jnp.zeros_like(adjoint_in))
    section_two, section_one = lax.fori_loop(0, SPIN_COLS // column_block, one_block, initial)
    return section_two, section_one
```

```python
import functools

import jax
import jax.numpy as jnp
from jax import lax
from jax.experimental import pallas as pl
from jax.experimental.pallas import tpu as pltpu
from jax.sharding import PartitionSpec as P

EXTENT_Z = 8
COLS = 4

flow_step = 0.0625
coef_late = 0.75 * flow_step
coef_mid = 8.0 / 9.0 * flow_step
MESH = pl.DeviceIdType.MESH


def mac(acc, link, vec, dagger):
    for r in range(3):
        for c in range(3):
            m_re = link(c, r, 0) if dagger else link(r, c, 0)
            m_im = link(c, r, 1) if dagger else link(r, c, 1)
            for j in range(COLS):
                v_re, v_im = vec[2 * c][j], vec[2 * c + 1][j]
                a_re = acc[2 * r][j] + m_re * v_re
                a_im = acc[2 * r + 1][j] + m_re * v_im
                if dagger:
                    acc[2 * r][j] = a_re + m_im * v_im
                    acc[2 * r + 1][j] = a_im - m_im * v_re
                else:
                    acc[2 * r][j] = a_re - m_im * v_im
                    acc[2 * r + 1][j] = a_im + m_im * v_re


def kernel(
    n_ta, n_sa,
    adj, late, mid, val, coord,
    two, one,
    top, inj, vals, keys, key_row, val_hi, val_lo,
    xh, ts, th, lts, lth, lxh, back,
    send, recv, lsend, lrecv, vsend, vrecv,
):
    ta, sa = lax.axis_index("ta"), lax.axis_index("sa")
    t_up, t_dn = lax.rem(ta + 1, n_ta), lax.rem(ta + n_ta - 1, n_ta)
    x_up, x_dn = lax.rem(sa + 1, n_sa), lax.rem(sa + n_sa - 1, n_sa)
    chunks = adj.shape[1] // COLS
    records = val.shape[1]
    planes = 2 * n_sa
    links = (late, mid)

    barrier = pltpu.get_barrier_semaphore()
    for step in range(1, n_sa):
        pl.semaphore_signal(
            barrier, inc=1, device_id={"sa": lax.rem(sa + step, n_sa)}, device_id_type=MESH
        )
    for other in (t_up, t_dn):
        pl.semaphore_signal(barrier, inc=1, device_id={"ta": other}, device_id_type=MESH)
    pl.semaphore_wait(barrier, n_sa + 1)

    def remote(src, dst, s, r, where):
        return pltpu.make_async_remote_copy(
            src_ref=src, dst_ref=dst, send_sem=s, recv_sem=r, device_id=where, device_id_type=MESH
        )

    def x_copy(lap, way, k):
        field = adj if lap == 0 else two
        cut = pl.ds(k * COLS, COLS)
        return remote(
            field.at[:, cut, way], xh.at[lap, way, :, cut],
            send.at[lap, way, k], recv.at[lap, way, k], {"sa": x_up if way else x_dn},
        )

    def t_copy(lap, way, k):
        return remote(
            ts.at[lap, way, k], th.at[lap, way, k],
            send.at[lap, 2 + way, k], recv.at[lap, 2 + way, k], {"ta": t_up if way else t_dn},
        )

    def lx_copy(lap):
        return remote(
            links[lap].at[1, :, 1], lxh.at[lap], lsend.at[lap, 0], lrecv.at[lap, 0], {"sa": x_up}
        )

    def lt_copy(lap):
        return remote(lts.at[lap], lth.at[lap], lsend.at[lap, 1], lrecv.at[lap, 1], {"ta": t_up})

    core = lax.rem(sa, 2)
    chip = sa // 2
    n_chip = n_sa // 2
    buddy = sa + 1 - 2 * core

    def rec_copies(kind, step):
        if kind == 0:
            peer = lax.rem(chip + step, n_chip) * 2 + core
            src_v, src_k = vals.at[0, 0], keys.at[0, 0]
        else:
            peer = buddy
            src_v, src_k = vals.at[0, step], keys.at[0, step]
        return (
            remote(src_v, vals.at[kind, step], vsend.at[kind, step, 0], vrecv.at[kind, step, 0], {"sa": peer}),
            remote(src_k, keys.at[kind, step], vsend.at[kind, step, 1], vrecv.at[kind, step, 1], {"sa": peer}),
        )

    vals[0, 0] = val[...]
    key = (coord[1:2, :] * 8 + coord[0:1, :] - ta * 8) * 128 + coord[2:3, :] * EXTENT_Z + coord[3:4, :]
    keys[0, 0] = jnp.broadcast_to(key, (8, records))
    for step in range(1, n_chip):
        for c in rec_copies(0, step):
            c.start()
    for c in rec_copies(1, 0):
        c.start()
    lx_copy(0).start()

    @pl.loop(0, chunks)
    def _(k):
        x_copy(0, 0, k).start()
        x_copy(0, 1, k).start()

    for lap in range(2):
        flat = links[lap].reshape(4 * 18 * 2 * 8, 128)
        lts[lap] = flat[pl.ds(7, 40, stride=8), :]
        lt_copy(lap).start()
    lx_copy(1).start()

    for step in range(1, n_chip):
        for c in rec_copies(0, step):
            c.wait_recv()
        for c in rec_copies(1, step):
            c.start()
    for step in range(n_chip):
        for c in rec_copies(1, step):
            c.wait_recv()
    for kind in range(2):
        for step in range(n_chip):
            at = (kind * n_chip + step) * records
            whole = vals[kind, step]
            high = whole.astype(jnp.bfloat16)
            val_hi[:, at : at + records] = high
            val_lo[:, at : at + records] = (whole - high.astype(jnp.float32)).astype(jnp.bfloat16)
            key_row[:, at : at + records] = keys[kind, step]

    top_flat = top.reshape(288 * 16, 128)
    adj_flat = adj.reshape(288 * 16, 128)
    width = key_row.shape[1]
    dims = (((1,), (1,)), ((), ()))

    @pl.loop(0, 4)
    def _(pair):
        for plane in range(4):
            if plane < 2:
                x_at = sa * 2 + plane
            elif plane == 2:
                x_at = x_up * 2
            else:
                x_at = x_dn * 2 + 1
            first = (x_at * 8 + pair * 2) * 128
            site = lax.broadcasted_iota(jnp.int32, (256, width), 0) + first
            hot = jnp.where(site == key_row[0:1, :], 1.0, 0.0).astype(jnp.bfloat16)
            got = lax.dot_general(val_hi[...], hot, dims, preferred_element_type=jnp.float32)
            got = got + lax.dot_general(val_lo[...], hot, dims, preferred_element_type=jnp.float32)
            for half in range(2):
                part = got[:, half * 128 : half * 128 + 128]
                t_at = pair * 2 + half
                if plane < 2:
                    rows = pl.ds(plane * 8 + t_at, 288, stride=16)
                    top_flat[rows, :] = adj_flat[rows, :] + part
                else:
                    inj.at[plane - 2].reshape(288 * 8, 128)[pl.ds(t_at, 288, stride=8), :] = part

    sign_dn = jnp.where(ta == 0, -1.0, 1.0).astype(jnp.float32)
    sign_up = jnp.where(ta == n_ta - 1, -1.0, 1.0).astype(jnp.float32)

    def send_time(lap, k):
        flat = (top if lap == 0 else two).reshape(288 * 16, 128)
        for comp in range(6):
            base = comp * 48 * 16 + k * COLS * 16
            ts[lap, 0, k, comp] = flat[pl.ds(base, 2 * COLS, stride=8), :] * sign_dn
            ts[lap, 1, k, comp] = flat[pl.ds(base + 7, 2 * COLS, stride=8), :] * sign_up
        t_copy(lap, 0, k).start()
        t_copy(lap, 1, k).start()

    @pl.loop(0, chunks)
    def _(k):
        send_time(0, k)

    row = lax.broadcasted_iota(jnp.int32, (8, 128), 0)
    z_at = lax.rem(lax.broadcasted_iota(jnp.int32, (8, 128), 1), EXTENT_Z)

    def y_ahead(a):
        return pltpu.roll(a, 128 - EXTENT_Z, 1)

    def y_behind(a):
        return pltpu.roll(a, EXTENT_Z, 1)

    def z_ahead(a):
        return jnp.where(z_at == EXTENT_Z - 1, pltpu.roll(a, EXTENT_Z - 1, 1), pltpu.roll(a, 127, 1))

    def z_behind(a):
        return jnp.where(z_at == 0, pltpu.roll(a, 129 - EXTENT_Z, 1), pltpu.roll(a, 1, 1))

    for lap in range(2):
        lx_copy(lap).wait_recv()
        lt_copy(lap).wait_recv()

        @pl.loop(0, 18)
        def _(e):
            link = links[lap]
            for x in range(2):
                edge = lth[lap, pl.ds(e * 2 + x, 1), :]
                back[lap, 0, e, x] = jnp.where(row == 0, edge, pltpu.roll(link[0, e, x], 1, 0))
                back[lap, 1, e, x] = lxh[lap, e] if x == 0 else link[1, e, 0]
                back[lap, 2, e, x] = y_behind(link[2, e, x])
                back[lap, 3, e, x] = z_behind(link[3, e, x])

    def laplacian(lap, k, x):
        field = top if lap == 0 else two
        link = links[lap]

        def ahead(mu):
            return lambda r, c, p: link[mu, (r * 3 + c) * 2 + p, x]

        def behind(mu):
            return lambda r, c, p: back[lap, mu, (r * 3 + c) * 2 + p, x]

        def here(plane):
            return [[field[q, k * COLS + j, plane] for j in range(COLS)] for q in range(6)]

        def halo(way):
            vec = [[xh[lap, way, q, k * COLS + j] for j in range(COLS)] for q in range(6)]
            if lap == 0:
                side = 0 if way == 0 else 1
                vec = [
                    [vec[q][j] + inj[side, q * 48 + k * COLS + j] for j in range(COLS)] for q in range(6)
                ]
            return vec

        def moved(f, vec):
            return [[f(a) for a in line] for line in vec]

        def time(way, vec):
            edge = 7 if way == 0 else 0
            turn = 7 if way == 0 else 1
            return [
                [
                    jnp.where(
                        row == edge,
                        th[lap, way, k, q, pl.ds(2 * j + x, 1), :],
                        pltpu.roll(vec[q][j], turn, 0),
                    )
                    for j in range(COLS)
                ]
                for q in range(6)
            ]

        centre = here(x)
        acc = [[-8.0 * a for a in line] for line in centre]
        mac(acc, ahead(2), moved(y_ahead, centre), False)
        mac(acc, behind(2), moved(y_behind, centre), True)
        mac(acc, ahead(3), moved(z_ahead, centre), False)
        mac(acc, behind(3), moved(z_behind, centre), True)
        mac(acc, ahead(0), time(0, centre), False)
        mac(acc, behind(0), time(1, centre), True)
        mac(acc, ahead(1), here(1) if x == 0 else halo(0), False)
        mac(acc, behind(1), halo(1) if x == 0 else here(0), True)
        return acc

    def arrive(lap, k):
        for way in range(2):
            x_copy(lap, way, k).wait_recv()
            t_copy(lap, way, k).wait_recv()

    @pl.loop(0, chunks)
    def _(k):
        arrive(0, k)
        for x in range(2):
            acc = laplacian(0, k, x)
            for q in range(6):
                for j in range(COLS):
                    two[q, k * COLS + j, x] = coef_late * acc[q][j]
        x_copy(1, 0, k).start()
        x_copy(1, 1, k).start()
        send_time(1, k)

    @pl.loop(0, chunks)
    def _(k):
        arrive(1, k)
        for x in range(2):
            acc = laplacian(1, k, x)
            for q in range(6):
                for j in range(COLS):
                    one[q, k * COLS + j, x] = top[q, k * COLS + j, x] + coef_mid * acc[q][j]

    for step in range(n_chip):
        for c in rec_copies(1, step):
            c.wait_send()
        if step:
            for c in rec_copies(0, step):
                c.wait_send()
    for lap in range(2):
        lx_copy(lap).wait_send()
        lt_copy(lap).wait_send()

        @pl.loop(0, chunks)
        def _(k):
            for way in range(2):
                x_copy(lap, way, k).wait_send()
                t_copy(lap, way, k).wait_send()


def shards(n_ta, n_sa, adjoint_in, links_late, links_mid, src_value, src_coord):
    cols = adjoint_in.shape[2]
    chunks = cols // COLS
    records = src_value.shape[3]
    f32 = jnp.float32
    adj = adjoint_in.reshape(6, cols, 2, 8, 128)
    late = links_late.reshape(4, 18, 2, 8, 128)
    mid = links_mid.reshape(4, 18, 2, 8, 128)
    val = src_value.reshape(6 * cols, records)
    width = n_sa * records
    dma = pltpu.SemaphoreType.DMA
    vmem = pl.BlockSpec(memory_space=pltpu.VMEM)
    two, one = pl.pallas_call(
        functools.partial(kernel, n_ta, n_sa),
        out_shape=(jax.ShapeDtypeStruct(adj.shape, f32), jax.ShapeDtypeStruct(adj.shape, f32)),
        in_specs=[vmem] * 5,
        out_specs=(vmem, vmem),
        scratch_shapes=[
            pltpu.VMEM(adj.shape, f32),
            pltpu.VMEM((2, 6 * cols, 8, 128), f32),
            pltpu.VMEM((2, n_sa // 2, 6 * cols, records), f32),
            pltpu.VMEM((2, n_sa // 2, 8, records), jnp.int32),
            pltpu.VMEM((8, width), jnp.int32),
            pltpu.VMEM((6 * cols, width), jnp.bfloat16),
            pltpu.VMEM((6 * cols, width), jnp.bfloat16),
            pltpu.VMEM((2, 2, 6, cols, 8, 128), f32),
            pltpu.VMEM((2, 2, chunks, 6, 2 * COLS, 128), f32),
            pltpu.VMEM((2, 2, chunks, 6, 2 * COLS, 128), f32),
            pltpu.VMEM((2, 40, 128), f32),
            pltpu.VMEM((2, 40, 128), f32),
            pltpu.VMEM((2, 18, 8, 128), f32),
            pltpu.VMEM((2, 4, 18, 2, 8, 128), f32),
            dma((2, 4, chunks)),
            dma((2, 4, chunks)),
            dma((2, 2)),
            dma((2, 2)),
            dma((2, n_sa // 2, 2)),
            dma((2, n_sa // 2, 2)),
        ],
        compiler_params=pltpu.CompilerParams(
            collective_id=0, has_side_effects=True, vmem_limit_bytes=52 * 1024 * 1024
        ),
    )(adj, late, mid, val, src_coord)
    return two.reshape(adjoint_in.shape), one.reshape(adjoint_in.shape)


def solution(mesh):
    return jax.shard_map(
        functools.partial(shards, mesh.shape["ta"], mesh.shape["sa"]),
        mesh=mesh,
        in_specs=(
            P(None, None, None, "sa", "ta", None),
            P(None, None, None, None, "sa", "ta", None),
            P(None, None, None, None, "sa", "ta", None),
            P(None, None, None, ("ta", "sa")),
            P(None, ("ta", "sa")),
        ),
        out_specs=(P(None, None, None, "sa", "ta", None), P(None, None, None, "sa", "ta", None)),
        check_vma=False,
    )
```

```python
import functools

import jax
import jax.numpy as jnp
from jax import lax
from jax.experimental import pallas as pl
from jax.experimental.pallas import tpu as pltpu
from jax.sharding import PartitionSpec as P

EXTENT_Z = 8
COLS = 4

flow_step = 0.0625
coef_late = 0.75 * flow_step
coef_mid = 8.0 / 9.0 * flow_step
MESH = pl.DeviceIdType.MESH


def mac(acc, link, vec, dagger):
    for r in range(3):
        for c in range(3):
            m_re = link(c, r, 0) if dagger else link(r, c, 0)
            m_im = link(c, r, 1) if dagger else link(r, c, 1)
            for j in range(COLS):
                v_re, v_im = vec[2 * c][j], vec[2 * c + 1][j]
                a_re = acc[2 * r][j] + m_re * v_re
                a_im = acc[2 * r + 1][j] + m_re * v_im
                if dagger:
                    acc[2 * r][j] = a_re + m_im * v_im
                    acc[2 * r + 1][j] = a_im - m_im * v_re
                else:
                    acc[2 * r][j] = a_re - m_im * v_im
                    acc[2 * r + 1][j] = a_im + m_im * v_re


def kernel(
    n_ta, n_sa,
    adj, late_in, mid_in, val, coord_in,
    two, one,
    top, late, mid, coord, inj, vals, keys, key_row, val_hi, val_lo,
    xh, xs, ts, th, lts, lth, back,
    send, recv, lsend, lrecv, vsend, vrecv, local,
):
    ta, sa = lax.axis_index("ta"), lax.axis_index("sa")
    t_up, t_dn = lax.rem(ta + 1, n_ta), lax.rem(ta + n_ta - 1, n_ta)
    x_up, x_dn = lax.rem(sa + 1, n_sa), lax.rem(sa + n_sa - 1, n_sa)
    chunks = adj.shape[1] // COLS
    records = val.shape[1]
    planes = 2 * n_sa
    links = (late, mid)

    loads = [
        pltpu.make_async_copy(src, dst, local.at[i])
        for i, (src, dst) in enumerate(
            ((coord_in, coord), (val, vals.at[0, 0]), (adj, top), (late_in, late), (mid_in, mid))
        )
    ]
    for load in loads:
        load.start()
    barrier = pltpu.get_barrier_semaphore()
    for step in range(1, n_sa):
        pl.semaphore_signal(
            barrier, inc=1, device_id={"sa": lax.rem(sa + step, n_sa)}, device_id_type=MESH
        )
    for other in (t_up, t_dn):
        pl.semaphore_signal(barrier, inc=1, device_id={"ta": other}, device_id_type=MESH)
    pl.semaphore_wait(barrier, n_sa + 1)

    def remote(src, dst, s, r, where):
        return pltpu.make_async_remote_copy(
            src_ref=src, dst_ref=dst, send_sem=s, recv_sem=r, device_id=where, device_id_type=MESH
        )

    def x_copy(lap, way, k):
        cut = pl.ds(k * COLS, COLS)
        if way == 1:
            src = xs.at[lap, :, cut]
        elif lap == 0:
            src = adj.at[:, cut, 0]
        else:
            src = two.at[:, cut, 0]
        return remote(
            src, xh.at[lap, way, :, cut],
            send.at[lap, way, k], recv.at[lap, way, k], {"sa": x_up if way else x_dn},
        )

    def t_copy(lap, way, k):
        return remote(
            ts.at[lap, way, k], th.at[lap, way, k],
            send.at[lap, 2 + way, k], recv.at[lap, 2 + way, k], {"ta": t_up if way else t_dn},
        )

    def lt_copy(lap):
        return remote(lts.at[lap], lth.at[lap], lsend.at[lap], lrecv.at[lap], {"ta": t_up})

    core = lax.rem(sa, 2)
    chip = sa // 2
    n_chip = n_sa // 2
    buddy = sa + 1 - 2 * core

    def rec_copies(kind, step):
        if kind == 0:
            peer = lax.rem(chip + step, n_chip) * 2 + core
            src_v, src_k = vals.at[0, 0], keys.at[0, 0]
        else:
            peer = buddy
            src_v, src_k = vals.at[0, step], keys.at[0, step]
        return (
            remote(src_v, vals.at[kind, step], vsend.at[kind, step, 0], vrecv.at[kind, step, 0], {"sa": peer}),
            remote(src_k, keys.at[kind, step], vsend.at[kind, step, 1], vrecv.at[kind, step, 1], {"sa": peer}),
        )

    loads[0].wait()
    key = (coord[1:2, :] * 8 + coord[0:1, :] - ta * 8) * 128 + coord[2:3, :] * EXTENT_Z + coord[3:4, :]
    keys[0, 0] = jnp.broadcast_to(key, (8, records))
    loads[1].wait()
    for step in range(1, n_chip):
        for c in rec_copies(0, step):
            c.start()
    for c in rec_copies(1, 0):
        c.start()

    @pl.loop(0, chunks // 3)
    def _(k):
        x_copy(0, 0, k).start()

    for load in loads[2:]:
        load.wait()
    for lap in range(2):
        flat = links[lap].reshape(4 * 18 * 2 * 8, 128)
        lts[lap] = flat[pl.ds(7, 40, stride=8), :]
        lt_copy(lap).start()

    for step in range(1, n_chip):
        for c in rec_copies(0, step):
            c.wait_recv()
        for c in rec_copies(1, step):
            c.start()

    @pl.loop(chunks // 3, chunks)
    def _(k):
        x_copy(0, 0, k).start()

    for step in range(n_chip):
        for c in rec_copies(1, step):
            c.wait_recv()
    for kind in range(2):
        for step in range(n_chip):
            at = (kind * n_chip + step) * records
            whole = vals[kind, step]
            high = whole.astype(jnp.bfloat16)
            val_hi[:, at : at + records] = high
            val_lo[:, at : at + records] = (whole - high.astype(jnp.float32)).astype(jnp.bfloat16)
            key_row[:, at : at + records] = keys[kind, step]

    top_flat = top.reshape(288 * 16, 128)
    width = key_row.shape[1]
    dims = (((1,), (1,)), ((), ()))

    @pl.loop(0, 4)
    def _(pair):
        for plane in range(3):
            x_at = sa * 2 + plane if plane < 2 else x_up * 2
            first = (x_at * 8 + pair * 2) * 128
            site = lax.broadcasted_iota(jnp.int32, (256, width), 0) + first
            hot = jnp.where(site == key_row[0:1, :], 1.0, 0.0).astype(jnp.bfloat16)
            got = lax.dot_general(val_hi[...], hot, dims, preferred_element_type=jnp.float32)
            got = got + lax.dot_general(val_lo[...], hot, dims, preferred_element_type=jnp.float32)
            for half in range(2):
                part = got[:, half * 128 : half * 128 + 128]
                t_at = pair * 2 + half
                if plane < 2:
                    rows = pl.ds(plane * 8 + t_at, 288, stride=16)
                    top_flat[rows, :] = top_flat[rows, :] + part
                else:
                    inj.reshape(288 * 8, 128)[pl.ds(t_at, 288, stride=8), :] = part

    sign_dn = jnp.where(ta == 0, -1.0, 1.0).astype(jnp.float32)
    sign_up = jnp.where(ta == n_ta - 1, -1.0, 1.0).astype(jnp.float32)

    def send_time(lap, k):
        flat = (top if lap == 0 else two).reshape(288 * 16, 128)
        for comp in range(6):
            base = comp * 48 * 16 + k * COLS * 16
            ts[lap, 0, k, comp] = flat[pl.ds(base, 2 * COLS, stride=8), :] * sign_dn
            ts[lap, 1, k, comp] = flat[pl.ds(base + 7, 2 * COLS, stride=8), :] * sign_up
        t_copy(lap, 0, k).start()
        t_copy(lap, 1, k).start()

    def send_back(lap, k):
        field, link = (top if lap == 0 else two), links[lap]
        vec = [[field[q, k * COLS + j, 1] for j in range(COLS)] for q in range(6)]
        acc = [[jnp.zeros((8, 128), jnp.float32)] * COLS for _ in range(6)]
        mac(acc, lambda r, c, p: link[1, (r * 3 + c) * 2 + p, 1], vec, True)
        for q in range(6):
            for j in range(COLS):
                xs[lap, q, k * COLS + j] = acc[q][j]
        x_copy(lap, 1, k).start()

    @pl.loop(0, chunks)
    def _(k):
        send_back(0, k)
        send_time(0, k)

    row = lax.broadcasted_iota(jnp.int32, (8, 128), 0)
    z_at = lax.rem(lax.broadcasted_iota(jnp.int32, (8, 128), 1), EXTENT_Z)

    def y_ahead(a):
        return pltpu.roll(a, 128 - EXTENT_Z, 1)

    def y_behind(a):
        return pltpu.roll(a, EXTENT_Z, 1)

    def z_ahead(a):
        return jnp.where(z_at == EXTENT_Z - 1, pltpu.roll(a, EXTENT_Z - 1, 1), pltpu.roll(a, 127, 1))

    def z_behind(a):
        return jnp.where(z_at == 0, pltpu.roll(a, 129 - EXTENT_Z, 1), pltpu.roll(a, 1, 1))

    for lap in range(2):
        lt_copy(lap).wait_recv()

        @pl.loop(0, 18)
        def _(e):
            link = links[lap]
            for x in range(2):
                edge = lth[lap, pl.ds(e * 2 + x, 1), :]
                back[lap, 0, e, x] = jnp.where(row == 0, edge, pltpu.roll(link[0, e, x], 1, 0))
                back[lap, 1, e, x] = y_behind(link[2, e, x])
                back[lap, 2, e, x] = z_behind(link[3, e, x])

    def laplacian(lap, k, x):
        field = top if lap == 0 else two
        link = links[lap]

        def ahead(mu):
            return lambda r, c, p: link[mu, (r * 3 + c) * 2 + p, x]

        def behind(which):
            return lambda r, c, p: back[lap, which, (r * 3 + c) * 2 + p, x]

        def here(plane):
            return [[field[q, k * COLS + j, plane] for j in range(COLS)] for q in range(6)]

        def halo(way):
            vec = [[xh[lap, way, q, k * COLS + j] for j in range(COLS)] for q in range(6)]
            if lap == 0 and way == 0:
                vec = [[vec[q][j] + inj[q * 48 + k * COLS + j] for j in range(COLS)] for q in range(6)]
            return vec

        def moved(f, vec):
            return [[f(a) for a in line] for line in vec]

        def time(way, vec):
            edge = 7 if way == 0 else 0
            turn = 7 if way == 0 else 1
            return [
                [
                    jnp.where(
                        row == edge,
                        th[lap, way, k, q, pl.ds(2 * j + x, 1), :],
                        pltpu.roll(vec[q][j], turn, 0),
                    )
                    for j in range(COLS)
                ]
                for q in range(6)
            ]

        centre = here(x)
        acc = [[-8.0 * a for a in line] for line in centre]
        mac(acc, ahead(2), moved(y_ahead, centre), False)
        mac(acc, behind(1), moved(y_behind, centre), True)
        mac(acc, ahead(3), moved(z_ahead, centre), False)
        mac(acc, behind(2), moved(z_behind, centre), True)
        mac(acc, ahead(0), time(0, centre), False)
        mac(acc, behind(0), time(1, centre), True)
        mac(acc, ahead(1), here(1) if x == 0 else halo(0), False)
        if x == 0:
            hop = halo(1)
            return [[acc[q][j] + hop[q][j] for j in range(COLS)] for q in range(6)]
        mac(acc, lambda r, c, p: link[1, (r * 3 + c) * 2 + p, 0], here(0), True)
        return acc

    def arrive(lap, k):
        for way in range(2):
            x_copy(lap, way, k).wait_recv()
            t_copy(lap, way, k).wait_recv()

    @pl.loop(0, chunks)
    def _(k):
        arrive(0, k)
        for x in range(2):
            acc = laplacian(0, k, x)
            for q in range(6):
                for j in range(COLS):
                    two[q, k * COLS + j, x] = coef_late * acc[q][j]
        x_copy(1, 0, k).start()
        send_back(1, k)
        send_time(1, k)

    @pl.loop(0, chunks)
    def _(k):
        arrive(1, k)
        for x in range(2):
            acc = laplacian(1, k, x)
            for q in range(6):
                for j in range(COLS):
                    one[q, k * COLS + j, x] = top[q, k * COLS + j, x] + coef_mid * acc[q][j]

    for step in range(n_chip):
        for c in rec_copies(1, step):
            c.wait_send()
        if step:
            for c in rec_copies(0, step):
                c.wait_send()
    for lap in range(2):
        lt_copy(lap).wait_send()

        @pl.loop(0, chunks)
        def _(k):
            for way in range(2):
                x_copy(lap, way, k).wait_send()
                t_copy(lap, way, k).wait_send()


def shards(n_ta, n_sa, adjoint_in, links_late, links_mid, src_value, src_coord):
    cols = adjoint_in.shape[2]
    chunks = cols // COLS
    records = src_value.shape[3]
    f32 = jnp.float32
    adj = adjoint_in.reshape(6, cols, 2, 8, 128)
    late = links_late.reshape(4, 18, 2, 8, 128)
    mid = links_mid.reshape(4, 18, 2, 8, 128)
    val = src_value.reshape(6 * cols, records)
    width = n_sa * records
    dma = pltpu.SemaphoreType.DMA
    vmem = pl.BlockSpec(memory_space=pltpu.VMEM)
    two, one = pl.pallas_call(
        functools.partial(kernel, n_ta, n_sa),
        out_shape=(pltpu.VMEM(adj.shape, f32), pltpu.VMEM(adj.shape, f32)),
        in_specs=[pl.BlockSpec(memory_space=pl.ANY)] * 5,
        out_specs=(vmem, vmem),
        scratch_shapes=[
            pltpu.VMEM(adj.shape, f32),
            pltpu.VMEM(late.shape, f32),
            pltpu.VMEM(mid.shape, f32),
            pltpu.VMEM(src_coord.shape, jnp.int32),
            pltpu.VMEM((6 * cols, 8, 128), f32),
            pltpu.VMEM((2, n_sa // 2, 6 * cols, records), f32),
            pltpu.VMEM((2, n_sa // 2, 8, records), jnp.int32),
            pltpu.VMEM((8, width), jnp.int32),
            pltpu.VMEM((6 * cols, width), jnp.bfloat16),
            pltpu.VMEM((6 * cols, width), jnp.bfloat16),
            pltpu.VMEM((2, 2, 6, cols, 8, 128), f32),
            pltpu.VMEM((2, 6, cols, 8, 128), f32),
            pltpu.VMEM((2, 2, chunks, 6, 2 * COLS, 128), f32),
            pltpu.VMEM((2, 2, chunks, 6, 2 * COLS, 128), f32),
            pltpu.VMEM((2, 40, 128), f32),
            pltpu.VMEM((2, 40, 128), f32),
            pltpu.VMEM((2, 3, 18, 2, 8, 128), f32),
            dma((2, 4, chunks)),
            dma((2, 4, chunks)),
            dma((2,)),
            dma((2,)),
            dma((2, n_sa // 2, 2)),
            dma((2, n_sa // 2, 2)),
            dma((5,)),
        ],
        compiler_params=pltpu.CompilerParams(
            collective_id=0, has_side_effects=True, vmem_limit_bytes=56 * 1024 * 1024
        ),
    )(adj, late, mid, val, src_coord)
    return two.reshape(adjoint_in.shape), one.reshape(adjoint_in.shape)


def solution(mesh):
    return jax.shard_map(
        functools.partial(shards, mesh.shape["ta"], mesh.shape["sa"]),
        mesh=mesh,
        in_specs=(
            P(None, None, None, "sa", "ta", None),
            P(None, None, None, None, "sa", "ta", None),
            P(None, None, None, None, "sa", "ta", None),
            P(None, None, None, ("ta", "sa")),
            P(None, ("ta", "sa")),
        ),
        out_specs=(P(None, None, None, "sa", "ta", None), P(None, None, None, "sa", "ta", None)),
        check_vma=False,
    )
```

```python
import functools

import jax
import jax.numpy as jnp
from jax import lax
from jax.experimental import pallas as pl
from jax.experimental.pallas import tpu as pltpu
from jax.sharding import PartitionSpec as P

EXTENT_Z = 8
COLS = 4

flow_step = 0.0625
coef_late = 0.75 * flow_step
coef_mid = 8.0 / 9.0 * flow_step
MESH = pl.DeviceIdType.MESH


def mac(acc, link, vec, dagger):
    for r in range(3):
        for c in range(3):
            m_re = link(c, r, 0) if dagger else link(r, c, 0)
            m_im = link(c, r, 1) if dagger else link(r, c, 1)
            for j in range(COLS):
                v_re, v_im = vec[2 * c][j], vec[2 * c + 1][j]
                a_re = acc[2 * r][j] + m_re * v_re
                a_im = acc[2 * r + 1][j] + m_re * v_im
                if dagger:
                    acc[2 * r][j] = a_re + m_im * v_im
                    acc[2 * r + 1][j] = a_im - m_im * v_re
                else:
                    acc[2 * r][j] = a_re - m_im * v_im
                    acc[2 * r + 1][j] = a_im + m_im * v_re


def kernel(
    n_ta, n_sa,
    adj, late_in, mid_in, val, coord_in,
    two, one,
    top, late, mid, coord, inj, vals, keys, key_row, val_hi, val_lo,
    xh, xs, ts, th, lts, lth, back,
    send, recv, lsend, lrecv, vsend, vrecv, local,
):
    ta, sa = lax.axis_index("ta"), lax.axis_index("sa")
    t_up, t_dn = lax.rem(ta + 1, n_ta), lax.rem(ta + n_ta - 1, n_ta)
    x_up, x_dn = lax.rem(sa + 1, n_sa), lax.rem(sa + n_sa - 1, n_sa)
    chunks = adj.shape[1] // COLS
    records = val.shape[1]
    planes = 2 * n_sa
    links = (late, mid)

    barrier = pltpu.get_barrier_semaphore()
    for step in range(1, n_sa):
        pl.semaphore_signal(
            barrier, inc=1, device_id={"sa": lax.rem(sa + step, n_sa)}, device_id_type=MESH
        )
    for other in (t_up, t_dn):
        pl.semaphore_signal(barrier, inc=1, device_id={"ta": other}, device_id_type=MESH)
    loads = [
        pltpu.make_async_copy(src, dst, local.at[i])
        for i, (src, dst) in enumerate(
            ((coord_in, coord), (val, vals.at[0, 0]), (adj, top), (late_in, late), (mid_in, mid))
        )
    ]
    for load in loads:
        load.start()
    pl.semaphore_wait(barrier, n_sa + 1)

    def remote(src, dst, s, r, where):
        return pltpu.make_async_remote_copy(
            src_ref=src, dst_ref=dst, send_sem=s, recv_sem=r, device_id=where, device_id_type=MESH
        )

    def x_copy(lap, way, k):
        cut = pl.ds(k * COLS, COLS)
        if way == 1:
            src = xs.at[lap, :, cut]
        elif lap == 0:
            src = adj.at[:, cut, 0]
        else:
            src = two.at[:, cut, 0]
        return remote(
            src, xh.at[lap, way, :, cut],
            send.at[lap, way, k], recv.at[lap, way, k], {"sa": x_up if way else x_dn},
        )

    def t_copy(lap, way, k):
        return remote(
            ts.at[lap, way, k], th.at[lap, way, k],
            send.at[lap, 2 + way, k], recv.at[lap, 2 + way, k], {"ta": t_up if way else t_dn},
        )

    def lt_copy(lap):
        return remote(lts.at[lap], lth.at[lap], lsend.at[lap], lrecv.at[lap], {"ta": t_up})

    core = lax.rem(sa, 2)
    chip = sa // 2
    n_chip = n_sa // 2
    buddy = sa + 1 - 2 * core

    def rec_copies(kind, step):
        if kind == 0:
            peer = lax.rem(chip + step, n_chip) * 2 + core
            src_v, src_k = vals.at[0, 0], keys.at[0, 0]
        else:
            peer = buddy
            src_v, src_k = vals.at[0, step], keys.at[0, step]
        return (
            remote(src_v, vals.at[kind, step], vsend.at[kind, step, 0], vrecv.at[kind, step, 0], {"sa": peer}),
            remote(src_k, keys.at[kind, step], vsend.at[kind, step, 1], vrecv.at[kind, step, 1], {"sa": peer}),
        )

    loads[0].wait()
    key = (coord[1:2, :] * 8 + coord[0:1, :] - ta * 8) * 128 + coord[2:3, :] * EXTENT_Z + coord[3:4, :]
    keys[0, 0] = jnp.broadcast_to(key, (8, records))
    loads[1].wait()
    for step in range(1, n_chip):
        for c in rec_copies(0, step):
            c.start()
    for c in rec_copies(1, 0):
        c.start()

    @pl.loop(0, chunks // 3)
    def _(k):
        x_copy(0, 0, k).start()

    for load in loads[2:]:
        load.wait()
    for lap in range(2):
        flat = links[lap].reshape(4 * 18 * 2 * 8, 128)
        lts[lap] = flat[pl.ds(7, 40, stride=8), :]
        lt_copy(lap).start()

    for step in range(1, n_chip):
        for c in rec_copies(0, step):
            c.wait_recv()
        for c in rec_copies(1, step):
            c.start()

    @pl.loop(chunks // 3, chunks)
    def _(k):
        x_copy(0, 0, k).start()

    for step in range(n_chip):
        for c in rec_copies(1, step):
            c.wait_recv()
    for kind in range(2):
        for step in range(n_chip):
            at = (kind * n_chip + step) * records
            whole = vals[kind, step]
            high = whole.astype(jnp.bfloat16)
            val_hi[:, at : at + records] = high
            val_lo[:, at : at + records] = (whole - high.astype(jnp.float32)).astype(jnp.bfloat16)
            key_row[:, at : at + records] = keys[kind, step]

    top_flat = top.reshape(288 * 16, 128)
    width = key_row.shape[1]
    dims = (((1,), (1,)), ((), ()))

    @pl.loop(0, 4)
    def _(pair):
        for plane in range(3):
            x_at = sa * 2 + plane if plane < 2 else x_up * 2
            first = (x_at * 8 + pair * 2) * 128
            site = lax.broadcasted_iota(jnp.int32, (256, width), 0) + first
            hot = jnp.where(site == key_row[0:1, :], 1.0, 0.0).astype(jnp.bfloat16)
            got = lax.dot_general(val_hi[...], hot, dims, preferred_element_type=jnp.float32)
            got = got + lax.dot_general(val_lo[...], hot, dims, preferred_element_type=jnp.float32)
            for half in range(2):
                part = got[:, half * 128 : half * 128 + 128]
                t_at = pair * 2 + half
                if plane < 2:
                    rows = pl.ds(plane * 8 + t_at, 288, stride=16)
                    top_flat[rows, :] = top_flat[rows, :] + part
                else:
                    inj.reshape(288 * 8, 128)[pl.ds(t_at, 288, stride=8), :] = part

    sign_dn = jnp.where(ta == 0, -1.0, 1.0).astype(jnp.float32)
    sign_up = jnp.where(ta == n_ta - 1, -1.0, 1.0).astype(jnp.float32)

    def send_time(lap, k):
        flat = (top if lap == 0 else two).reshape(288 * 16, 128)
        for comp in range(6):
            base = comp * 48 * 16 + k * COLS * 16
            ts[lap, 0, k, comp] = flat[pl.ds(base, 2 * COLS, stride=8), :] * sign_dn
            ts[lap, 1, k, comp] = flat[pl.ds(base + 7, 2 * COLS, stride=8), :] * sign_up
        t_copy(lap, 0, k).start()
        t_copy(lap, 1, k).start()

    def send_back(lap, k):
        field, link = (top if lap == 0 else two), links[lap]
        vec = [[field[q, k * COLS + j, 1] for j in range(COLS)] for q in range(6)]
        acc = [[jnp.zeros((8, 128), jnp.float32)] * COLS for _ in range(6)]
        mac(acc, lambda r, c, p: link[1, (r * 3 + c) * 2 + p, 1], vec, True)
        for q in range(6):
            for j in range(COLS):
                xs[lap, q, k * COLS + j] = acc[q][j]
        x_copy(lap, 1, k).start()

    @pl.loop(0, chunks)
    def _(k):
        send_back(0, k)
        send_time(0, k)

    row = lax.broadcasted_iota(jnp.int32, (8, 128), 0)
    z_at = lax.rem(lax.broadcasted_iota(jnp.int32, (8, 128), 1), EXTENT_Z)

    def y_ahead(a):
        return pltpu.roll(a, 128 - EXTENT_Z, 1)

    def y_behind(a):
        return pltpu.roll(a, EXTENT_Z, 1)

    def z_ahead(a):
        return jnp.where(z_at == EXTENT_Z - 1, pltpu.roll(a, EXTENT_Z - 1, 1), pltpu.roll(a, 127, 1))

    def z_behind(a):
        return jnp.where(z_at == 0, pltpu.roll(a, 129 - EXTENT_Z, 1), pltpu.roll(a, 1, 1))

    for lap in range(2):
        lt_copy(lap).wait_recv()

        @pl.loop(0, 18)
        def _(e):
            link = links[lap]
            for x in range(2):
                edge = lth[lap, pl.ds(e * 2 + x, 1), :]
                back[lap, 0, e, x] = jnp.where(row == 0, edge, pltpu.roll(link[0, e, x], 1, 0))
                back[lap, 1, e, x] = y_behind(link[2, e, x])
                back[lap, 2, e, x] = z_behind(link[3, e, x])

    def laplacian(lap, k, x):
        field = top if lap == 0 else two
        link = links[lap]

        def ahead(mu):
            return lambda r, c, p: link[mu, (r * 3 + c) * 2 + p, x]

        def behind(which):
            return lambda r, c, p: back[lap, which, (r * 3 + c) * 2 + p, x]

        def here(plane):
            return [[field[q, k * COLS + j, plane] for j in range(COLS)] for q in range(6)]

        def halo(way):
            vec = [[xh[lap, way, q, k * COLS + j] for j in range(COLS)] for q in range(6)]
            if lap == 0 and way == 0:
                vec = [[vec[q][j] + inj[q * 48 + k * COLS + j] for j in range(COLS)] for q in range(6)]
            return vec

        def moved(f, vec):
            return [[f(a) for a in line] for line in vec]

        def time(way, vec):
            edge = 7 if way == 0 else 0
            turn = 7 if way == 0 else 1
            return [
                [
                    jnp.where(
                        row == edge,
                        th[lap, way, k, q, pl.ds(2 * j + x, 1), :],
                        pltpu.roll(vec[q][j], turn, 0),
                    )
                    for j in range(COLS)
                ]
                for q in range(6)
            ]

        centre = here(x)
        acc = [[-8.0 * a for a in line] for line in centre]
        mac(acc, ahead(2), moved(y_ahead, centre), False)
        mac(acc, behind(1), moved(y_behind, centre), True)
        mac(acc, ahead(3), moved(z_ahead, centre), False)
        mac(acc, behind(2), moved(z_behind, centre), True)
        mac(acc, ahead(0), time(0, centre), False)
        mac(acc, behind(0), time(1, centre), True)
        mac(acc, ahead(1), here(1) if x == 0 else halo(0), False)
        if x == 0:
            hop = halo(1)
            return [[acc[q][j] + hop[q][j] for j in range(COLS)] for q in range(6)]
        mac(acc, lambda r, c, p: link[1, (r * 3 + c) * 2 + p, 0], here(0), True)
        return acc

    def arrive(lap, k):
        for way in range(2):
            x_copy(lap, way, k).wait_recv()
            t_copy(lap, way, k).wait_recv()

    @pl.loop(0, chunks)
    def _(k):
        arrive(0, k)
        for x in range(2):
            acc = laplacian(0, k, x)
            for q in range(6):
                for j in range(COLS):
                    two[q, k * COLS + j, x] = coef_late * acc[q][j]
        x_copy(1, 0, k).start()
        send_back(1, k)
        send_time(1, k)

    @pl.loop(0, chunks)
    def _(k):
        arrive(1, k)
        for x in range(2):
            acc = laplacian(1, k, x)
            for q in range(6):
                for j in range(COLS):
                    one[q, k * COLS + j, x] = top[q, k * COLS + j, x] + coef_mid * acc[q][j]

    for step in range(n_chip):
        for c in rec_copies(1, step):
            c.wait_send()
        if step:
            for c in rec_copies(0, step):
                c.wait_send()
    for lap in range(2):
        lt_copy(lap).wait_send()

        @pl.loop(0, chunks)
        def _(k):
            for way in range(2):
                x_copy(lap, way, k).wait_send()
                t_copy(lap, way, k).wait_send()


def shards(n_ta, n_sa, adjoint_in, links_late, links_mid, src_value, src_coord):
    cols = adjoint_in.shape[2]
    chunks = cols // COLS
    records = src_value.shape[3]
    f32 = jnp.float32
    adj = adjoint_in.reshape(6, cols, 2, 8, 128)
    late = links_late.reshape(4, 18, 2, 8, 128)
    mid = links_mid.reshape(4, 18, 2, 8, 128)
    val = src_value.reshape(6 * cols, records)
    width = n_sa * records
    dma = pltpu.SemaphoreType.DMA
    vmem = pl.BlockSpec(memory_space=pltpu.VMEM)
    two, one = pl.pallas_call(
        functools.partial(kernel, n_ta, n_sa),
        out_shape=(pltpu.VMEM(adj.shape, f32), pltpu.VMEM(adj.shape, f32)),
        in_specs=[pl.BlockSpec(memory_space=pl.ANY)] * 5,
        out_specs=(vmem, vmem),
        scratch_shapes=[
            pltpu.VMEM(adj.shape, f32),
            pltpu.VMEM(late.shape, f32),
            pltpu.VMEM(mid.shape, f32),
            pltpu.VMEM(src_coord.shape, jnp.int32),
            pltpu.VMEM((6 * cols, 8, 128), f32),
            pltpu.VMEM((2, n_sa // 2, 6 * cols, records), f32),
            pltpu.VMEM((2, n_sa // 2, 8, records), jnp.int32),
            pltpu.VMEM((8, width), jnp.int32),
            pltpu.VMEM((6 * cols, width), jnp.bfloat16),
            pltpu.VMEM((6 * cols, width), jnp.bfloat16),
            pltpu.VMEM((2, 2, 6, cols, 8, 128), f32),
            pltpu.VMEM((2, 6, cols, 8, 128), f32),
            pltpu.VMEM((2, 2, chunks, 6, 2 * COLS, 128), f32),
            pltpu.VMEM((2, 2, chunks, 6, 2 * COLS, 128), f32),
            pltpu.VMEM((2, 40, 128), f32),
            pltpu.VMEM((2, 40, 128), f32),
            pltpu.VMEM((2, 3, 18, 2, 8, 128), f32),
            dma((2, 4, chunks)),
            dma((2, 4, chunks)),
            dma((2,)),
            dma((2,)),
            dma((2, n_sa // 2, 2)),
            dma((2, n_sa // 2, 2)),
            dma((5,)),
        ],
        compiler_params=pltpu.CompilerParams(
            collective_id=0, has_side_effects=True, vmem_limit_bytes=56 * 1024 * 1024
        ),
    )(adj, late, mid, val, src_coord)
    def write_out(two_ref, one_ref, two_out, one_out, sem):
        copies = [
            pltpu.make_async_copy(src.at[q], dst.at[q], sem.at[i, q])
            for q in range(6)
            for i, (src, dst) in enumerate(((two_ref, two_out), (one_ref, one_out)))
        ]
        for c in copies:
            c.start()
        for c in copies:
            c.wait()

    out = jax.ShapeDtypeStruct(adj.shape, f32)
    hbm = pl.BlockSpec(memory_space=pl.ANY)
    two, one = pl.pallas_call(
        write_out,
        out_shape=(out, out),
        in_specs=[vmem, vmem],
        out_specs=(hbm, hbm),
        scratch_shapes=[dma((2, 6))],
        compiler_params=pltpu.CompilerParams(vmem_limit_bytes=1024 * 1024),
    )(two, one)
    return two.reshape(adjoint_in.shape), one.reshape(adjoint_in.shape)


def solution(mesh):
    return jax.shard_map(
        functools.partial(shards, mesh.shape["ta"], mesh.shape["sa"]),
        mesh=mesh,
        in_specs=(
            P(None, None, None, "sa", "ta", None),
            P(None, None, None, None, "sa", "ta", None),
            P(None, None, None, None, "sa", "ta", None),
            P(None, None, None, ("ta", "sa")),
            P(None, ("ta", "sa")),
        ),
        out_specs=(P(None, None, None, "sa", "ta", None), P(None, None, None, "sa", "ta", None)),
        check_vma=False,
    )
```
